32 devices in a mesh: slab: 16 (over z, y, x), col: 2 (over core).
Axes of the slice: x: 2, y: 2, z: 4, core: 2. Of those that a mesh axis runs over, the one named last changes fastest.
Arguments:
- diagonal_tiles: float32 [64, 128, 128], P(('slab', 'col')), as said below
- lower_tiles: float32 [64, 128, 128], P(('slab', 'col')), may hold values from -0.109375 to 0.109375
- upper_tiles: float32 [64, 128, 128], P(('slab', 'col')), may hold values from -0.109375 to 0.109375
- tile_pattern: int32 [64, 2], P(('slab', 'col')), may hold values 0 or 1
- interface_ids: int32 [8192], P('slab'), may hold values from 0 to 4095
- coupling_values: float32 [8192], P('slab'), may hold values from -1.5 to 1.5
- warm_start: float32 [8192, 512], P('slab', 'col'), may hold values from -6 to 6
- boundary_stiffness: float32 [512, 512], P('slab', 'col'), may hold values from -6 to 6
Outputs:
- constraint_modes: float32 [8192, 512], P('slab', 'col')
- reduced_stiffness: float32 [512, 512], P('slab', 'col')
The draws below stay inside these ranges and needn't reach their ends.
Inputs may be any that keep to these rules, and one draw needn't show every extreme that they name: `interface_ids`: values of 512 or more mark rows coupled to no interface column. `diagonal_tiles`: every tile is symmetric positive definite.
All inputs are finite; a program needn't handle non-finite values. No bound on the sum of `tile_pattern` on one device may be relied on, other than what follows from the above.
Results may differ from the reference program's by a relative error of at most 0.00017.
Values sent between devices are 32-bit elements; how exact they have to be, the bound alone decides.
A program may use at most 64 MiB of HBM per device.

```python
import math
import jax
import jax.numpy as jnp
from jax import lax

IFACE = 512
TILE = 128
SWEEPS = 2
NBLK = 64
ROWS = 8192


def draw_diagonal_tiles(key, part):
    key_off = jax.random.fold_in(key, 11)
    key_diag = jax.random.fold_in(key, 12)
    spread = 1.6 / math.sqrt(TILE)
    offset = jax.random.uniform(key_off, (NBLK, TILE, TILE), jnp.float32, -spread, spread)
    symmetric = 0.5 * (offset + jnp.swapaxes(offset, 1, 2))
    top = 1.5
    levels = 1.45 + jnp.exp(jax.random.uniform(key_diag, (NBLK, TILE), jnp.float32, math.log(0.05), math.log(top)))
    rows_index = jnp.arange(TILE)[:, None]
    cols_index = jnp.arange(TILE)[None, :]
    return jnp.where((rows_index == cols_index)[None, :, :], levels[:, :, None], symmetric)


def with_ends(values, stream_key, low, largest):
    index_at = [jax.random.randint(jax.random.fold_in(stream_key, axis), (), 0, length) for axis, length in enumerate(values.shape)]
    longest = values.shape.index(max(values.shape))
    beside = index_at[:longest] + [(index_at[longest] + 1) % values.shape[longest]] + index_at[longest + 1:]
    return values.at[tuple(index_at)].set(low).at[tuple(beside)].set(largest)


def shard_levels(key, extent, split, least, high):
    gain = 1.0
    for axis_at, blocks in split:
        steps = jax.random.uniform(jax.random.fold_in(jax.random.fold_in(key, 6), axis_at), (blocks,), jnp.float32, least / len(split), high / len(split))
        gain = gain * jnp.repeat(jnp.exp(steps), extent[axis_at] // blocks).reshape((-1,) + (1,) * (len(extent) - 1 - axis_at))
    return gain


def noise(key, extent, scale, most, pieces=(), kind=jnp.bfloat16):
    level = shard_levels(key, extent, pieces, -0.22, 0.18) if pieces else 1.0
    array = jax.random.normal(key, extent, jnp.float32) * scale * level
    return jnp.minimum(jnp.maximum(array, -most), most).astype(kind)


def setup_inputs(seed: int = 0) -> dict:
    arg_keys = jax.random.split(jax.random.key(seed), 9)
    diagonal_tiles = draw_diagonal_tiles(jax.random.fold_in(arg_keys[8], 71), 0)
    lower_tiles = noise(arg_keys[1], (NBLK, TILE, TILE), (25 * TILE) ** -0.5, 0.109375, ((0, 32),), jnp.float32)
    upper_tiles = noise(arg_keys[2], (NBLK, TILE, TILE), (25 * TILE) ** -0.5, 0.109375, ((0, 32),), jnp.float32)
    tile_pattern = with_ends((jax.random.randint(arg_keys[3], (NBLK, 2), 0, 4) < 3).astype(jnp.int32), jax.random.fold_in(arg_keys[3], 1), 0, 1)
    interface_ids = with_ends(jax.random.randint(arg_keys[4], (ROWS,), 0, 8 * IFACE), jax.random.fold_in(arg_keys[4], 1), 0, (8 * IFACE) - 1).astype(jnp.int32)
    coupling_values = noise(arg_keys[5], (ROWS,), 0.25, 1.5, ((0, 16),), jnp.float32)
    warm_start = noise(arg_keys[6], (ROWS, IFACE), 1.0, 6.0, ((0, 16), (1, 2)), jnp.float32)
    boundary_stiffness = noise(arg_keys[7], (IFACE, IFACE), 1.0, 6.0, ((0, 16), (1, 2)), jnp.float32)
    return dict(diagonal_tiles=diagonal_tiles, lower_tiles=lower_tiles, upper_tiles=upper_tiles, tile_pattern=tile_pattern, interface_ids=interface_ids, coupling_values=coupling_values, warm_start=warm_start, boundary_stiffness=boundary_stiffness)


def tile_inverse(factors):
    count = factors.shape[0]
    size = factors.shape[1]
    identity = jnp.broadcast_to(jnp.eye(size, dtype=jnp.float32), (count, size, size))
    inner = lax.linalg.triangular_solve(factors, identity, left_side=True, lower=True)
    return lax.linalg.triangular_solve(factors, inner, left_side=True, lower=True, transpose_a=True)

def reference(diagonal_tiles, lower_tiles, upper_tiles, tile_pattern, interface_ids, coupling_values, warm_start, boundary_stiffness):
    present = tile_pattern.astype(jnp.float32)
    lower_masked = lower_tiles * present[:, 0][:, None, None]
    upper_masked = upper_tiles * present[:, 1][:, None, None]
    factors = jnp.linalg.cholesky(diagonal_tiles)
    inverses = tile_inverse(factors)
    group = min(128, IFACE)
    groups = IFACE // group
    columns = jnp.arange(IFACE, dtype=jnp.int32)
    right_side = jnp.where(interface_ids[:, None] == columns[None, :], -coupling_values[:, None], jnp.float32(0.0))
    rhs_groups = right_side.reshape(NBLK, TILE, groups, group).transpose(2, 0, 1, 3)
    warm_groups = warm_start.reshape(NBLK, TILE, groups, group).transpose(2, 0, 1, 3)

    def run_group(pair):
        rhs, modes = pair
        empty = jnp.zeros((1, TILE, group), jnp.float32)
        for step in range(SWEEPS):
            below = jnp.concatenate([empty, modes[:-1]], axis=0)
            above = jnp.concatenate([modes[1:], empty], axis=0)
            residual = rhs - jnp.einsum('bij,bjc->bic', lower_masked, below, precision=lax.Precision.HIGHEST)
            residual = residual - jnp.einsum('bij,bjc->bic', upper_masked, above, precision=lax.Precision.HIGHEST)
            modes = jnp.einsum('bij,bjc->bic', inverses, residual, precision=lax.Precision.HIGHEST)
        return modes
    result = lax.map(run_group, (rhs_groups, warm_groups))
    constraint_modes = result.transpose(1, 2, 0, 3).reshape(ROWS, IFACE)
    weight = jnp.where(interface_ids < IFACE, coupling_values, jnp.float32(0.0))
    target = jnp.minimum(interface_ids, IFACE - 1).astype(jnp.int32)
    summed = jax.ops.segment_sum(weight[:, None] * constraint_modes, target, num_segments=IFACE)
    return (constraint_modes, boundary_stiffness + summed)
```

```python
import functools

import jax
import jax.numpy as jnp
from jax import lax
from jax.experimental import pallas as pl
from jax.experimental.pallas import tpu as pltpu
from jax.sharding import PartitionSpec as P

IFACE = 512
TILE = 128
SWEEPS = 2
NEAR = 4
HIGH = lax.Precision.HIGHEST
MESH = pl.DeviceIdType.MESH


def tile_inverse(factors):
    count = factors.shape[0]
    size = factors.shape[1]
    identity = jnp.broadcast_to(jnp.eye(size, dtype=jnp.float32), (count, size, size))
    inner = lax.linalg.triangular_solve(factors, identity, left_side=True, lower=True)
    return lax.linalg.triangular_solve(factors, inner, left_side=True, lower=True, transpose_a=True)


def dot(a, b):
    return jnp.dot(a, b, precision=HIGH, preferred_element_type=jnp.float32)


def body(
    slabs,
    reduce_here,
    pattern_ref,
    inv_in,
    lower_ref,
    upper_ref,
    ids_ref,
    values_ref,
    warm_ref,
    boundary_ref,
    modes_ref,
    reduced_ref,
    lu,
    inv,
    halo,
    mid,
    parts,
    near_in,
    far_out,
    far_in,
    pair_send,
    pair_recv,
    halo_send,
    halo_recv,
    near_send,
    near_recv,
    far_send,
    far_recv,
):
    slab, col = lax.axis_index("slab"), lax.axis_index("col")
    here = lower_ref.shape[0]
    blocks = 2 * here
    width = warm_ref.shape[1]
    other = (slab, 1 - col)
    far = slabs // NEAR
    owned = IFACE // slabs
    hi, lo = slab // NEAR, lax.rem(slab, NEAR)
    near_ids = [(hi * NEAR + lax.rem(lo + k, NEAR), col) for k in range(1, NEAR)]
    far_ids = [(lax.rem(hi + k, far) * NEAR + lo, col) for k in range(1, far)]
    is_first, is_last = slab == 0, slab == slabs - 1

    barrier = pltpu.get_barrier_semaphore()
    steps = range(1, slabs) if reduce_here else (1, slabs - 1)
    partners = [other] + [(lax.rem(slab + k, slabs), col) for k in steps]
    for partner in partners:
        pl.semaphore_signal(barrier, inc=1, device_id=partner, device_id_type=MESH)

    for b in range(here):
        at = col * here + b
        lu[at, :, :TILE] = lower_ref[b] * pattern_ref[b, 0].astype(jnp.float32)
        lu[at, :, TILE:] = upper_ref[b] * pattern_ref[b, 1].astype(jnp.float32)
        inv[at] = inv_in[b]

    pl.semaphore_wait(barrier, len(partners))

    def halos(step, first_block, last_block):
        down = pltpu.make_async_remote_copy(
            src_ref=first_block,
            dst_ref=halo.at[2 * step + 1],
            send_sem=halo_send.at[2 * step],
            recv_sem=halo_recv.at[2 * step + 1],
            device_id=(slab - 1, col),
            device_id_type=MESH,
        )
        up = pltpu.make_async_remote_copy(
            src_ref=last_block,
            dst_ref=halo.at[2 * step],
            send_sem=halo_send.at[2 * step + 1],
            recv_sem=halo_recv.at[2 * step],
            device_id=(slab + 1, col),
            device_id_type=MESH,
        )
        return down, up

    def start_halos(copies):
        down, up = copies

        @pl.when(jnp.logical_not(is_first))
        def _():
            down.start()

        @pl.when(jnp.logical_not(is_last))
        def _():
            up.start()

    def wait_halos(step, copies):
        down, up = copies

        @pl.when(jnp.logical_not(is_first))
        def _():
            down.wait_send()
            up.wait_recv()

        @pl.when(is_first)
        def _():
            halo[2 * step] = jnp.zeros((TILE, width), jnp.float32)

        @pl.when(jnp.logical_not(is_last))
        def _():
            up.wait_send()
            down.wait_recv()

        @pl.when(is_last)
        def _():
            halo[2 * step + 1] = jnp.zeros((TILE, width), jnp.float32)

    def pair(ref, which):
        mine = ref.at[pl.ds(col * here, here)]
        return pltpu.make_async_remote_copy(
            src_ref=mine,
            dst_ref=mine,
            send_sem=pair_send.at[which],
            recv_sem=pair_recv.at[which],
            device_id=other,
            device_id_type=MESH,
        )

    warm_halos = halos(0, warm_ref.at[pl.ds(0, TILE)], warm_ref.at[pl.ds((blocks - 1) * TILE, TILE)])
    start_halos(warm_halos)
    tiles = pair(lu, 0)
    tiles.start()
    inverses = pair(inv, 1)
    inverses.start()

    rows = blocks * TILE
    ids_row = jnp.minimum(ids_ref[...], IFACE).astype(jnp.float32)
    values_row = values_ref[...]
    ids_col = jnp.broadcast_to(ids_row, (8, rows)).T[:, :1].astype(jnp.int32)
    values_col = jnp.broadcast_to(values_row, (8, rows)).T[:, :1]
    columns = lax.broadcasted_iota(jnp.int32, (TILE, width), 1) + col * width

    def right_side(b):
        part = slice(b * TILE, (b + 1) * TILE)
        return jnp.where(ids_col[part] == columns, -values_col[part], 0.0)

    tiles.wait()
    inverses.wait()

    def update(b, below, above):
        both = jnp.concatenate([below, above], axis=0)
        return dot(inv[b], right_side(b) - dot(lu[b], both))

    def old(ref, step, b):
        if b < 0:
            return halo[2 * step]
        if b >= blocks:
            return halo[2 * step + 1]
        return ref[b * TILE : (b + 1) * TILE, :]

    wait_halos(0, warm_halos)
    mid_halos = halos(1, mid.at[pl.ds(0, TILE)], mid.at[pl.ds((blocks - 1) * TILE, TILE)])
    order = [0, blocks - 1] + list(range(1, blocks - 1))
    for n, b in enumerate(order):
        mid[b * TILE : (b + 1) * TILE, :] = update(b, old(warm_ref, 0, b - 1), old(warm_ref, 0, b + 1))
        if n == 1:
            start_halos(mid_halos)
    for n, b in enumerate(order[2:] + order[:2]):
        if n == blocks - 2:
            wait_halos(1, mid_halos)
        modes_ref[b * TILE : (b + 1) * TILE, :] = update(b, old(mid, 1, b - 1), old(mid, 1, b + 1))

    ids_now = ids_row.astype(jnp.int32)
    modes = modes_ref[...]
    group = IFACE // NEAR
    index = lax.broadcasted_iota(jnp.int32, (group, rows), 0)

    def share(target):
        chosen = jnp.where(index_target(target) == ids_now, values_row, 0.0)
        return dot(chosen, modes)

    def index_target(target):
        if not reduce_here:
            return index + target * group
        return (index // owned) * (NEAR * owned) + target * owned + lax.rem(index, owned)

    if not reduce_here:
        for k in range(NEAR):
            reduced_ref[k * group : (k + 1) * group, :] = share(k)
        return

    sent = []
    for k in range(1, NEAR):
        parts[k - 1] = share(lax.rem(lo + k, NEAR))
        copy = pltpu.make_async_remote_copy(
            src_ref=parts.at[k - 1],
            dst_ref=near_in.at[k - 1],
            send_sem=near_send.at[k - 1],
            recv_sem=near_recv.at[k - 1],
            device_id=near_ids[k - 1],
            device_id_type=MESH,
        )
        copy.start()
        sent.append(copy)
    total = share(lo)
    for k, copy in enumerate(sent):
        copy.wait()
        total = total + near_in[k]
    far_out[...] = total.reshape(far, owned, width)
    sent = []
    for k in range(1, far):
        copy = pltpu.make_async_remote_copy(
            src_ref=far_out.at[lax.rem(hi + k, far)],
            dst_ref=far_in.at[k - 1],
            send_sem=far_send.at[k - 1],
            recv_sem=far_recv.at[k - 1],
            device_id=far_ids[k - 1],
            device_id_type=MESH,
        )
        copy.start()
        sent.append(copy)
    result = boundary_ref[...] + far_out[hi]
    for k, copy in enumerate(sent):
        copy.wait()
        result = result + far_in[k]
    reduced_ref[...] = result


def on_device(
    diagonal_tiles,
    lower_tiles,
    upper_tiles,
    tile_pattern,
    interface_ids,
    coupling_values,
    warm_start,
    boundary_stiffness,
):
    slabs = lax.axis_size("slab")
    here = diagonal_tiles.shape[0]
    rows, width = warm_start.shape
    owned = boundary_stiffness.shape[0]
    reduce_here = slabs % NEAR == 0 and slabs > NEAR and owned % 8 == 0
    far = slabs // NEAR if reduce_here else 2
    inverses = tile_inverse(jnp.linalg.cholesky(diagonal_tiles))
    vmem = pl.BlockSpec(memory_space=pltpu.VMEM)
    f32 = jnp.float32
    sem = pltpu.SemaphoreType.DMA
    modes, reduced = pl.pallas_call(
        functools.partial(body, slabs, reduce_here),
        out_shape=(
            jax.ShapeDtypeStruct((rows, width), f32),
            jax.ShapeDtypeStruct((owned if reduce_here else IFACE, width), f32),
        ),
        in_specs=[pl.BlockSpec(memory_space=pltpu.SMEM)] + [vmem] * 7,
        out_specs=(vmem, vmem),
        scratch_shapes=[
            pltpu.VMEM((2 * here, TILE, 2 * TILE), f32),
            pltpu.VMEM((2 * here, TILE, TILE), f32),
            pltpu.VMEM((2 * SWEEPS, TILE, width), f32),
            pltpu.VMEM((rows, width), f32),
            pltpu.VMEM((NEAR - 1, IFACE // NEAR, width), f32),
            pltpu.VMEM((NEAR - 1, IFACE // NEAR, width), f32),
            pltpu.VMEM((far, owned, width), f32),
            pltpu.VMEM((far - 1, owned, width), f32),
            sem((2,)),
            sem((2,)),
            sem((2 * SWEEPS,)),
            sem((2 * SWEEPS,)),
            sem((NEAR - 1,)),
            sem((NEAR - 1,)),
            sem((far - 1,)),
            sem((far - 1,)),
        ],
        compiler_params=pltpu.CompilerParams(
            collective_id=0, has_side_effects=True, vmem_limit_bytes=40 * 1024 * 1024
        ),
    )(
        tile_pattern,
        inverses,
        lower_tiles,
        upper_tiles,
        interface_ids.reshape(1, rows),
        coupling_values.reshape(1, rows),
        warm_start,
        boundary_stiffness,
    )
    if not reduce_here:
        total = lax.psum(reduced, "slab")
        share = lax.dynamic_slice_in_dim(total, lax.axis_index("slab") * owned, owned)
        reduced = boundary_stiffness + share
    return (modes, reduced)


def solution(mesh):
    placed = (
        P(("slab", "col"), None, None),
        P(("slab", "col"), None, None),
        P(("slab", "col"), None, None),
        P(("slab", "col"), None),
        P("slab"),
        P("slab"),
        P("slab", "col"),
        P("slab", "col"),
    )
    return jax.shard_map(
        on_device,
        mesh=mesh,
        in_specs=placed,
        out_specs=(P("slab", "col"), P("slab", "col")),
        check_vma=False,
    )
```

```python
import functools

import jax
import jax.numpy as jnp
from jax import lax
from jax.experimental import pallas as pl
from jax.experimental.pallas import tpu as pltpu
from jax.sharding import PartitionSpec as P

IFACE = 512
TILE = 128
SWEEPS = 2
NEAR = 4
SUB = 8
HIGH = lax.Precision.HIGHEST
MESH = pl.DeviceIdType.MESH


def swept(block):
    size = len(block)
    e = {(i, j): block[i][j] for i in range(size) for j in range(i, size)}
    for k in range(size):
        r = 1.0 / e[k, k]
        c = [e[min(i, k), max(i, k)] for i in range(size)]
        t = [x * r for x in c]
        for i in range(size):
            for j in range(i, size):
                if i == k and j == k:
                    e[i, j] = -r
                elif i == k:
                    e[i, j] = t[j]
                elif j == k:
                    e[i, j] = t[i]
                else:
                    e[i, j] = e[i, j] - c[i] * t[j]
    return e


def sweep_rows(ref, at, k):
    first = pl.multiple_of(k * SUB, SUB)
    panel = ref[at, pl.ds(first, SUB), :]
    corner = pltpu.roll(panel, lax.rem(TILE - k * SUB, TILE), 1)
    lanes = lax.broadcasted_iota(jnp.int32, (SUB, TILE), 1) - k * SUB
    subs = lax.broadcasted_iota(jnp.int32, (SUB, TILE), 0)
    wide = [jnp.broadcast_to(corner[:, j : j + 1], (SUB, TILE)) for j in range(SUB)]
    table = [
        [jnp.broadcast_to(wide[j][i : i + 1, :], (SUB, TILE)) if j >= i else None for j in range(SUB)]
        for i in range(SUB)
    ]
    e = swept(table)
    inside = (lanes >= 0) & (lanes < SUB)
    source = jnp.where(inside, jnp.where(lanes == subs, 1.0, 0.0), -panel)
    rows = None
    for j in range(SUB):
        column = e[0, j]
        for i in range(1, SUB):
            column = jnp.where(subs == i, e[min(i, j), max(i, j)], column)
        term = column * jnp.broadcast_to(source[j : j + 1, :], (SUB, TILE))
        rows = term if rows is None else rows + term
    change = lax.dot_general(
        panel, rows, (((0,), (0,)), ((), ())), precision=HIGH, preferred_element_type=jnp.float32
    )
    full = lax.broadcasted_iota(jnp.int32, (TILE, TILE), 1) - k * SUB
    ref[at] = jnp.where((full >= 0) & (full < SUB), 0.0, ref[at]) - change
    ref[at, pl.ds(first, SUB), :] = rows


def dot(a, b):
    return jnp.dot(a, b, precision=HIGH, preferred_element_type=jnp.float32)


def body(
    slabs,
    reduce_here,
    pattern_ref,
    diagonal_ref,
    lower_ref,
    upper_ref,
    ids_ref,
    values_ref,
    warm_ref,
    boundary_ref,
    modes_ref,
    reduced_ref,
    lu,
    inv,
    halo,
    mid,
    parts,
    near_in,
    far_out,
    far_in,
    pair_send,
    pair_recv,
    halo_send,
    halo_recv,
    near_send,
    near_recv,
    far_send,
    far_recv,
):
    slab, col = lax.axis_index("slab"), lax.axis_index("col")
    here = lower_ref.shape[0]
    blocks = 2 * here
    width = warm_ref.shape[1]
    other = (slab, 1 - col)
    far = slabs // NEAR
    owned = IFACE // slabs
    hi, lo = slab // NEAR, lax.rem(slab, NEAR)
    near_ids = [(hi * NEAR + lax.rem(lo + k, NEAR), col) for k in range(1, NEAR)]
    far_ids = [(lax.rem(hi + k, far) * NEAR + lo, col) for k in range(1, far)]
    is_first, is_last = slab == 0, slab == slabs - 1

    barrier = pltpu.get_barrier_semaphore()
    steps = range(1, slabs) if reduce_here else (1, slabs - 1)
    partners = [other] + [(lax.rem(slab + k, slabs), col) for k in steps]
    for partner in partners:
        pl.semaphore_signal(barrier, inc=1, device_id=partner, device_id_type=MESH)

    for b in range(here):
        at = col * here + b
        lu[at, :, :TILE] = lower_ref[b] * pattern_ref[b, 0].astype(jnp.float32)
        lu[at, :, TILE:] = upper_ref[b] * pattern_ref[b, 1].astype(jnp.float32)
        inv[at] = diagonal_ref[b]

    pl.semaphore_wait(barrier, len(partners))

    def halos(step, first_block, last_block):
        down = pltpu.make_async_remote_copy(
            src_ref=first_block,
            dst_ref=halo.at[2 * step + 1],
            send_sem=halo_send.at[2 * step],
            recv_sem=halo_recv.at[2 * step + 1],
            device_id=(slab - 1, col),
            device_id_type=MESH,
        )
        up = pltpu.make_async_remote_copy(
            src_ref=last_block,
            dst_ref=halo.at[2 * step],
            send_sem=halo_send.at[2 * step + 1],
            recv_sem=halo_recv.at[2 * step],
            device_id=(slab + 1, col),
            device_id_type=MESH,
        )
        return down, up

    def start_halos(copies):
        down, up = copies

        @pl.when(jnp.logical_not(is_first))
        def _():
            down.start()

        @pl.when(jnp.logical_not(is_last))
        def _():
            up.start()

    def wait_halos(step, copies):
        down, up = copies

        @pl.when(jnp.logical_not(is_first))
        def _():
            down.wait_send()
            up.wait_recv()

        @pl.when(is_first)
        def _():
            halo[2 * step] = jnp.zeros((TILE, width), jnp.float32)

        @pl.when(jnp.logical_not(is_last))
        def _():
            up.wait_send()
            down.wait_recv()

        @pl.when(is_last)
        def _():
            halo[2 * step + 1] = jnp.zeros((TILE, width), jnp.float32)

    def pair(ref, which):
        mine = ref.at[pl.ds(col * here, here)]
        return pltpu.make_async_remote_copy(
            src_ref=mine,
            dst_ref=mine,
            send_sem=pair_send.at[which],
            recv_sem=pair_recv.at[which],
            device_id=other,
            device_id_type=MESH,
        )

    warm_halos = halos(0, warm_ref.at[pl.ds(0, TILE)], warm_ref.at[pl.ds((blocks - 1) * TILE, TILE)])
    start_halos(warm_halos)
    tiles = pair(lu, 0)
    tiles.start()
    rows = blocks * TILE
    ids_row = jnp.minimum(ids_ref[...], IFACE).astype(jnp.float32)
    values_row = values_ref[...]
    ids_col = jnp.broadcast_to(ids_row, (8, rows)).T[:, :1].astype(jnp.int32)
    values_col = jnp.broadcast_to(values_row, (8, rows)).T[:, :1]
    columns = lax.broadcasted_iota(jnp.int32, (TILE, width), 1) + col * width

    def right_side(b):
        part = slice(b * TILE, (b + 1) * TILE)
        return jnp.where(ids_col[part] == columns, -values_col[part], 0.0)

    def invert(k, carry):
        for b in range(here):
            sweep_rows(inv, col * here + b, k)
        return carry

    lax.fori_loop(0, TILE // SUB, invert, 0)
    inverses = pair(inv, 1)
    inverses.start()
    tiles.wait()
    inverses.wait()

    def update(b, below, above):
        both = jnp.concatenate([below, above], axis=0)
        return dot(inv[b], dot(lu[b], both) - right_side(b))

    def old(ref, step, b):
        if b < 0:
            return halo[2 * step]
        if b >= blocks:
            return halo[2 * step + 1]
        return ref[b * TILE : (b + 1) * TILE, :]

    wait_halos(0, warm_halos)
    mid_halos = halos(1, mid.at[pl.ds(0, TILE)], mid.at[pl.ds((blocks - 1) * TILE, TILE)])
    order = [0, blocks - 1] + list(range(1, blocks - 1))
    for n, b in enumerate(order):
        mid[b * TILE : (b + 1) * TILE, :] = update(b, old(warm_ref, 0, b - 1), old(warm_ref, 0, b + 1))
        if n == 1:
            start_halos(mid_halos)
    for n, b in enumerate(order[2:] + order[:2]):
        if n == blocks - 2:
            wait_halos(1, mid_halos)
        modes_ref[b * TILE : (b + 1) * TILE, :] = update(b, old(mid, 1, b - 1), old(mid, 1, b + 1))

    ids_now = ids_row.astype(jnp.int32)
    modes = modes_ref[...]
    group = IFACE // NEAR
    index = lax.broadcasted_iota(jnp.int32, (group, rows), 0)

    def share(target):
        chosen = jnp.where(index_target(target) == ids_now, values_row, 0.0)
        return dot(chosen, modes)

    def index_target(target):
        if not reduce_here:
            return index + target * group
        return (index // owned) * (NEAR * owned) + target * owned + lax.rem(index, owned)

    if not reduce_here:
        for k in range(NEAR):
            reduced_ref[k * group : (k + 1) * group, :] = share(k)
        return

    sent = []
    for k in range(1, NEAR):
        parts[k - 1] = share(lax.rem(lo + k, NEAR))
        copy = pltpu.make_async_remote_copy(
            src_ref=parts.at[k - 1],
            dst_ref=near_in.at[k - 1],
            send_sem=near_send.at[k - 1],
            recv_sem=near_recv.at[k - 1],
            device_id=near_ids[k - 1],
            device_id_type=MESH,
        )
        copy.start()
        sent.append(copy)
    total = share(lo)
    for k, copy in enumerate(sent):
        copy.wait()
        total = total + near_in[k]
    far_out[...] = total.reshape(far, owned, width)
    sent = []
    for k in range(1, far):
        copy = pltpu.make_async_remote_copy(
            src_ref=far_out.at[lax.rem(hi + k, far)],
            dst_ref=far_in.at[k - 1],
            send_sem=far_send.at[k - 1],
            recv_sem=far_recv.at[k - 1],
            device_id=far_ids[k - 1],
            device_id_type=MESH,
        )
        copy.start()
        sent.append(copy)
    result = boundary_ref[...] + far_out[hi]
    for k, copy in enumerate(sent):
        copy.wait()
        result = result + far_in[k]
    reduced_ref[...] = result


def on_device(
    diagonal_tiles,
    lower_tiles,
    upper_tiles,
    tile_pattern,
    interface_ids,
    coupling_values,
    warm_start,
    boundary_stiffness,
):
    slabs = lax.axis_size("slab")
    here = diagonal_tiles.shape[0]
    rows, width = warm_start.shape
    owned = boundary_stiffness.shape[0]
    reduce_here = slabs % NEAR == 0 and slabs > NEAR and owned % 8 == 0
    far = slabs // NEAR if reduce_here else 2
    vmem = pl.BlockSpec(memory_space=pltpu.VMEM)
    f32 = jnp.float32
    sem = pltpu.SemaphoreType.DMA
    modes, reduced = pl.pallas_call(
        functools.partial(body, slabs, reduce_here),
        out_shape=(
            jax.ShapeDtypeStruct((rows, width), f32),
            jax.ShapeDtypeStruct((owned if reduce_here else IFACE, width), f32),
        ),
        in_specs=[pl.BlockSpec(memory_space=pltpu.SMEM)] + [vmem] * 7,
        out_specs=(vmem, vmem),
        scratch_shapes=[
            pltpu.VMEM((2 * here, TILE, 2 * TILE), f32),
            pltpu.VMEM((2 * here, TILE, TILE), f32),
            pltpu.VMEM((2 * SWEEPS, TILE, width), f32),
            pltpu.VMEM((rows, width), f32),
            pltpu.VMEM((NEAR - 1, IFACE // NEAR, width), f32),
            pltpu.VMEM((NEAR - 1, IFACE // NEAR, width), f32),
            pltpu.VMEM((far, owned, width), f32),
            pltpu.VMEM((far - 1, owned, width), f32),
            sem((2,)),
            sem((2,)),
            sem((2 * SWEEPS,)),
            sem((2 * SWEEPS,)),
            sem((NEAR - 1,)),
            sem((NEAR - 1,)),
            sem((far - 1,)),
            sem((far - 1,)),
        ],
        compiler_params=pltpu.CompilerParams(
            collective_id=0, has_side_effects=True, vmem_limit_bytes=40 * 1024 * 1024
        ),
    )(
        tile_pattern,
        diagonal_tiles,
        lower_tiles,
        upper_tiles,
        interface_ids.reshape(1, rows),
        coupling_values.reshape(1, rows),
        warm_start,
        boundary_stiffness,
    )
    if not reduce_here:
        total = lax.psum(reduced, "slab")
        share = lax.dynamic_slice_in_dim(total, lax.axis_index("slab") * owned, owned)
        reduced = boundary_stiffness + share
    return (modes, reduced)


def solution(mesh):
    placed = (
        P(("slab", "col"), None, None),
        P(("slab", "col"), None, None),
        P(("slab", "col"), None, None),
        P(("slab", "col"), None),
        P("slab"),
        P("slab"),
        P("slab", "col"),
        P("slab", "col"),
    )
    return jax.shard_map(
        on_device,
        mesh=mesh,
        in_specs=placed,
        out_specs=(P("slab", "col"), P("slab", "col")),
        check_vma=False,
    )
```

```python
import functools

import jax
import jax.numpy as jnp
from jax import lax
from jax.experimental import pallas as pl
from jax.experimental.pallas import tpu as pltpu
from jax.sharding import PartitionSpec as P

IFACE = 512
TILE = 128
SWEEPS = 2
NEAR = 4
SUB = 8
MESH = pl.DeviceIdType.MESH


def pieces(x, count):
    out = []
    for _ in range(count):
        piece = x.astype(jnp.bfloat16).astype(jnp.float32)
        out.append(piece)
        x = x - piece
    return out


def swept(columns, subs):
    tiles = range(len(columns))
    for k in range(SUB):
        pivots = [[jnp.broadcast_to(columns[t][k][j : j + 1, :], (SUB, TILE)) for j in range(SUB)] for t in tiles]
        inverted = [1.0 / pivots[t][k] for t in tiles]
        scaled = [columns[t][k] * inverted[t] for t in tiles]
        here = subs == k
        new = []
        for t in tiles:
            new.append(
                [
                    jnp.where(here, -inverted[t], scaled[t])
                    if j == k
                    else jnp.where(here, pivots[t][j] * inverted[t], columns[t][j] - scaled[t] * pivots[t][j])
                    for j in range(SUB)
                ]
            )
        columns = new
    return columns


def sweep_rows(ref, base, count, k):
    first = pl.multiple_of(k * SUB, SUB)
    tiles = range(count)
    lanes = lax.broadcasted_iota(jnp.int32, (SUB, TILE), 1) - k * SUB
    subs = lax.broadcasted_iota(jnp.int32, (SUB, TILE), 0)
    inside = (lanes >= 0) & (lanes < SUB)
    unit = jnp.where(lanes == subs, 1.0, 0.0)
    full = lax.broadcasted_iota(jnp.int32, (TILE, TILE), 1) - k * SUB
    outside = (full < 0) | (full >= SUB)
    panels = [ref[base + t, pl.ds(first, SUB), :] for t in tiles]
    shift = lax.rem(TILE - k * SUB, TILE)
    corners = [pltpu.roll(panels[t], shift, 1) for t in tiles]
    columns = [
        [jnp.broadcast_to(corners[t][:, j : j + 1], (SUB, TILE)) for j in range(SUB)] for t in tiles
    ]
    left = []
    for t in tiles:
        a1, a2, a3 = pieces(panels[t], 3)
        left.append(jnp.concatenate([a1, a1, a2, a1, a2, a3], axis=0).astype(jnp.bfloat16))
    columns = swept(columns, subs)
    rows = []
    for t in tiles:
        source = jnp.where(inside, unit, -panels[t])
        terms = [columns[t][j] * jnp.broadcast_to(source[j : j + 1, :], (SUB, TILE)) for j in range(SUB)]
        while len(terms) > 1:
            terms = [terms[i] + terms[i + 1] for i in range(0, len(terms), 2)]
        rows.append(terms[0])
    changes = []
    for t in tiles:
        b1, b2, b3 = pieces(rows[t], 3)
        right = jnp.concatenate([b1, b2, b1, b3, b2, b1], axis=0).astype(jnp.bfloat16)
        changes.append(
            lax.dot_general(left[t], right, (((0,), (0,)), ((), ())), preferred_element_type=jnp.float32)
        )
    for t in tiles:
        ref[base + t] = jnp.where(outside, ref[base + t], 0.0) - changes[t]
        ref[base + t, pl.ds(first, SUB), :] = rows[t]


def split(x):
    high = x.astype(jnp.bfloat16)
    return high, (x - high.astype(jnp.float32)).astype(jnp.bfloat16)


def product(a, b):
    return jnp.dot(a, b, preferred_element_type=jnp.float32)


def dot(a, b):
    (ah, al), (bh, bl) = split(a), split(b)
    return product(ah, bh) + (product(ah, bl) + product(al, bh))


def body(
    slabs,
    reduce_here,
    pattern_ref,
    diagonal_hbm,
    lower_hbm,
    upper_hbm,
    ids_hbm,
    values_hbm,
    warm_hbm,
    boundary_hbm,
    modes_hbm,
    reduced_hbm,
    lower_ref,
    upper_ref,
    ids_ref,
    values_ref,
    warm_ref,
    boundary_ref,
    modes_ref,
    reduced_ref,
    local,
    lu,
    inv,
    halo,
    mid,
    parts,
    near_in,
    far_out,
    far_in,
    pair_send,
    pair_recv,
    halo_send,
    halo_recv,
    near_send,
    near_recv,
    far_send,
    far_recv,
):
    slab, col = lax.axis_index("slab"), lax.axis_index("col")
    here = lower_ref.shape[0]
    blocks = 2 * here
    width = warm_ref.shape[1]
    other = (slab, 1 - col)
    far = slabs // NEAR
    owned = IFACE // slabs
    hi, lo = slab // NEAR, lax.rem(slab, NEAR)
    near_ids = [(hi * NEAR + lax.rem(lo + k, NEAR), col) for k in range(1, NEAR)]
    far_ids = [(lax.rem(hi + k, far) * NEAR + lo, col) for k in range(1, far)]
    is_first, is_last = slab == 0, slab == slabs - 1

    barrier = pltpu.get_barrier_semaphore()
    steps = range(1, slabs) if reduce_here else (1, slabs - 1)
    partners = [other] + [(lax.rem(slab + k, slabs), col) for k in steps]
    for partner in partners:
        pl.semaphore_signal(barrier, inc=1, device_id=partner, device_id_type=MESH)

    mine = pl.ds(col * here, here)
    sources = [lower_hbm, upper_hbm, diagonal_hbm, warm_hbm, ids_hbm, values_hbm, boundary_hbm]
    places = [lower_ref, upper_ref, inv.at[mine], warm_ref, ids_ref, values_ref, boundary_ref]
    loads = [
        pltpu.make_async_copy(source, place, local.at[i])
        for i, (source, place) in enumerate(zip(sources, places))
    ]
    for load in loads:
        load.start()
    loads[0].wait()
    loads[1].wait()
    for b in range(here):
        at = col * here + b
        lu[at, :, :TILE] = lower_ref[b] * pattern_ref[b, 0].astype(jnp.float32)
        lu[at, :, TILE:] = upper_ref[b] * pattern_ref[b, 1].astype(jnp.float32)

    pl.semaphore_wait(barrier, len(partners))

    def halos(step, first_block, last_block):
        down = pltpu.make_async_remote_copy(
            src_ref=first_block,
            dst_ref=halo.at[2 * step + 1],
            send_sem=halo_send.at[2 * step],
            recv_sem=halo_recv.at[2 * step + 1],
            device_id=(slab - 1, col),
            device_id_type=MESH,
        )
        up = pltpu.make_async_remote_copy(
            src_ref=last_block,
            dst_ref=halo.at[2 * step],
            send_sem=halo_send.at[2 * step + 1],
            recv_sem=halo_recv.at[2 * step],
            device_id=(slab + 1, col),
            device_id_type=MESH,
        )
        return down, up

    def start_halos(copies):
        down, up = copies

        @pl.when(jnp.logical_not(is_first))
        def _():
            down.start()

        @pl.when(jnp.logical_not(is_last))
        def _():
            up.start()

    def wait_halos(step, copies):
        down, up = copies

        @pl.when(jnp.logical_not(is_first))
        def _():
            down.wait_send()
            up.wait_recv()

        @pl.when(is_first)
        def _():
            halo[2 * step] = jnp.zeros((TILE, width), jnp.float32)

        @pl.when(jnp.logical_not(is_last))
        def _():
            up.wait_send()
            down.wait_recv()

        @pl.when(is_last)
        def _():
            halo[2 * step + 1] = jnp.zeros((TILE, width), jnp.float32)

    def pair(ref, which):
        part = ref.at[mine]
        return pltpu.make_async_remote_copy(
            src_ref=part,
            dst_ref=part,
            send_sem=pair_send.at[which],
            recv_sem=pair_recv.at[which],
            device_id=other,
            device_id_type=MESH,
        )

    warm_halos = halos(0, warm_hbm.at[pl.ds(0, TILE)], warm_hbm.at[pl.ds((blocks - 1) * TILE, TILE)])
    start_halos(warm_halos)
    tiles = pair(lu, 0)
    tiles.start()
    rows = blocks * TILE
    loads[2].wait()

    def invert(k, carry):
        sweep_rows(inv, col * here, here, k)
        return carry

    lax.fori_loop(0, TILE // SUB, invert, 0)
    inverses = pair(inv, 1)
    inverses.start()

    for load in loads[3:]:
        load.wait()
    ids_row = jnp.minimum(ids_ref[...], IFACE).astype(jnp.float32)
    ids_col = jnp.broadcast_to(ids_row, (8, rows)).T[:, :1].astype(jnp.int32)
    values_col = jnp.broadcast_to(values_ref[...], (8, rows)).T[:, :1]
    columns = lax.broadcasted_iota(jnp.int32, (TILE, width), 1) + col * width

    def right_side(b):
        part = slice(b * TILE, (b + 1) * TILE)
        return jnp.where(ids_col[part] == columns, -values_col[part], 0.0)

    def residual(b, below, above):
        both = jnp.concatenate([below, above], axis=0)
        return dot(lu[b], both) - right_side(b)

    def old(ref, step, b):
        if b < 0:
            return halo[2 * step]
        if b >= blocks:
            return halo[2 * step + 1]
        return ref[b * TILE : (b + 1) * TILE, :]

    tiles.wait()
    wait_halos(0, warm_halos)
    mid_halos = halos(1, mid.at[pl.ds(0, TILE)], mid.at[pl.ds((blocks - 1) * TILE, TILE)])
    order = [0, blocks - 1] + list(range(1, blocks - 1))
    held = [residual(b, old(warm_ref, 0, b - 1), old(warm_ref, 0, b + 1)) for b in order]
    inverses.wait()
    for n, b in enumerate(order):
        mid[b * TILE : (b + 1) * TILE, :] = dot(inv[b], held[n])
        if n == 1:
            start_halos(mid_halos)
    stores = []
    for n, b in enumerate(order[2:] + order[:2]):
        if n == blocks - 2:
            wait_halos(1, mid_halos)
        part = pl.ds(b * TILE, TILE)
        modes_ref[part, :] = dot(inv[b], residual(b, old(mid, 1, b - 1), old(mid, 1, b + 1)))
        store = pltpu.make_async_copy(modes_ref.at[part], modes_hbm.at[part], local.at[len(loads) + n])
        store.start()
        stores.append(store)

    ids_now = ids_row.astype(jnp.int32)
    weighted_high, weighted_low = split(values_col * modes_ref[...])
    group = IFACE // NEAR
    index = lax.broadcasted_iota(jnp.int32, (group, rows), 0)

    def share(target):
        chosen = jnp.where(index_target(target) == ids_now, 1.0, 0.0).astype(jnp.bfloat16)
        return product(chosen, weighted_high) + product(chosen, weighted_low)

    def index_target(target):
        if not reduce_here:
            return index + target * group
        return (index // owned) * (NEAR * owned) + target * owned + lax.rem(index, owned)

    def finish():
        last = pltpu.make_async_copy(reduced_ref, reduced_hbm, local.at[len(loads) + blocks])
        last.start()
        for store in stores + [last]:
            store.wait()

    if not reduce_here:
        for k in range(NEAR):
            reduced_ref[k * group : (k + 1) * group, :] = share(k)
        finish()
        return

    sent = []
    for k in range(1, NEAR):
        parts[k - 1] = share(lax.rem(lo + k, NEAR))
        copy = pltpu.make_async_remote_copy(
            src_ref=parts.at[k - 1],
            dst_ref=near_in.at[k - 1],
            send_sem=near_send.at[k - 1],
            recv_sem=near_recv.at[k - 1],
            device_id=near_ids[k - 1],
            device_id_type=MESH,
        )
        copy.start()
        sent.append(copy)
    total = share(lo)
    for k, copy in enumerate(sent):
        copy.wait()
        total = total + near_in[k]
    far_out[...] = total.reshape(far, owned, width)
    sent = []
    for k in range(1, far):
        copy = pltpu.make_async_remote_copy(
            src_ref=far_out.at[lax.rem(hi + k, far)],
            dst_ref=far_in.at[k - 1],
            send_sem=far_send.at[k - 1],
            recv_sem=far_recv.at[k - 1],
            device_id=far_ids[k - 1],
            device_id_type=MESH,
        )
        copy.start()
        sent.append(copy)
    result = boundary_ref[...] + far_out[hi]
    for k, copy in enumerate(sent):
        copy.wait()
        result = result + far_in[k]
    reduced_ref[...] = result
    finish()


def on_device(
    diagonal_tiles,
    lower_tiles,
    upper_tiles,
    tile_pattern,
    interface_ids,
    coupling_values,
    warm_start,
    boundary_stiffness,
):
    slabs = lax.axis_size("slab")
    here = diagonal_tiles.shape[0]
    rows, width = warm_start.shape
    owned = boundary_stiffness.shape[0]
    reduce_here = slabs % NEAR == 0 and slabs > NEAR and owned % 8 == 0
    far = slabs // NEAR if reduce_here else 2
    hbm = pl.BlockSpec(memory_space=pl.ANY)
    f32 = jnp.float32
    sem = pltpu.SemaphoreType.DMA
    modes, reduced = pl.pallas_call(
        functools.partial(body, slabs, reduce_here),
        out_shape=(
            jax.ShapeDtypeStruct((rows, width), f32),
            jax.ShapeDtypeStruct((owned if reduce_here else IFACE, width), f32),
        ),
        in_specs=[pl.BlockSpec(memory_space=pltpu.SMEM)] + [hbm] * 7,
        out_specs=(hbm, hbm),
        scratch_shapes=[
            pltpu.VMEM((here, TILE, TILE), f32),
            pltpu.VMEM((here, TILE, TILE), f32),
            pltpu.VMEM((1, rows), jnp.int32),
            pltpu.VMEM((1, rows), f32),
            pltpu.VMEM((rows, width), f32),
            pltpu.VMEM((owned, width), f32),
            pltpu.VMEM((rows, width), f32),
            pltpu.VMEM((owned if reduce_here else IFACE, width), f32),
            sem((8 + 2 * here,)),
            pltpu.VMEM((2 * here, TILE, 2 * TILE), f32),
            pltpu.VMEM((2 * here, TILE, TILE), f32),
            pltpu.VMEM((2 * SWEEPS, TILE, width), f32),
            pltpu.VMEM((rows, width), f32),
            pltpu.VMEM((NEAR - 1, IFACE // NEAR, width), f32),
            pltpu.VMEM((NEAR - 1, IFACE // NEAR, width), f32),
            pltpu.VMEM((far, owned, width), f32),
            pltpu.VMEM((far - 1, owned, width), f32),
            sem((2,)),
            sem((2,)),
            sem((2 * SWEEPS,)),
            sem((2 * SWEEPS,)),
            sem((NEAR - 1,)),
            sem((NEAR - 1,)),
            sem((far - 1,)),
            sem((far - 1,)),
        ],
        compiler_params=pltpu.CompilerParams(
            collective_id=0, has_side_effects=True, vmem_limit_bytes=40 * 1024 * 1024
        ),
    )(
        tile_pattern,
        diagonal_tiles,
        lower_tiles,
        upper_tiles,
        interface_ids.reshape(1, rows),
        coupling_values.reshape(1, rows),
        warm_start,
        boundary_stiffness,
    )
    if not reduce_here:
        total = lax.psum(reduced, "slab")
        share = lax.dynamic_slice_in_dim(total, lax.axis_index("slab") * owned, owned)
        reduced = boundary_stiffness + share
    return (modes, reduced)


def solution(mesh):
    placed = (
        P(("slab", "col"), None, None),
        P(("slab", "col"), None, None),
        P(("slab", "col"), None, None),
        P(("slab", "col"), None),
        P("slab"),
        P("slab"),
        P("slab", "col"),
        P("slab", "col"),
    )
    return jax.shard_map(
        on_device,
        mesh=mesh,
        in_specs=placed,
        out_specs=(P("slab", "col"), P("slab", "col")),
        check_vma=False,
    )
```

```python
import functools

import jax
import jax.numpy as jnp
from jax import lax
from jax.experimental import pallas as pl
from jax.experimental.pallas import tpu as pltpu
from jax.sharding import PartitionSpec as P

IFACE = 512
TILE = 128
SWEEPS = 2
NEAR = 4
SUB = 8
MESH = pl.DeviceIdType.MESH


def pieces(x, count):
    out = []
    for _ in range(count):
        piece = x.astype(jnp.bfloat16).astype(jnp.float32)
        out.append(piece)
        x = x - piece
    return out


def swept(columns, subs):
    tiles = range(len(columns))
    for k in range(SUB):
        pivots = [[jnp.broadcast_to(columns[t][k][j : j + 1, :], (SUB, TILE)) for j in range(SUB)] for t in tiles]
        inverted = [1.0 / pivots[t][k] for t in tiles]
        scaled = [columns[t][k] * inverted[t] for t in tiles]
        here = subs == k
        new = []
        for t in tiles:
            new.append(
                [
                    jnp.where(here, -inverted[t], scaled[t])
                    if j == k
                    else jnp.where(here, pivots[t][j] * inverted[t], columns[t][j] - scaled[t] * pivots[t][j])
                    for j in range(SUB)
                ]
            )
        columns = new
    return columns


def sweep_rows(ref, base, count, k):
    first = pl.multiple_of(k * SUB, SUB)
    tiles = range(count)
    lanes = lax.broadcasted_iota(jnp.int32, (SUB, TILE), 1) - k * SUB
    subs = lax.broadcasted_iota(jnp.int32, (SUB, TILE), 0)
    inside = (lanes >= 0) & (lanes < SUB)
    unit = jnp.where(lanes == subs, 1.0, 0.0)
    full = lax.broadcasted_iota(jnp.int32, (TILE, TILE), 1) - k * SUB
    outside = (full < 0) | (full >= SUB)
    panels = [ref[base + t, pl.ds(first, SUB), :] for t in tiles]
    shift = lax.rem(TILE - k * SUB, TILE)
    corners = [pltpu.roll(panels[t], shift, 1) for t in tiles]
    columns = [
        [jnp.broadcast_to(corners[t][:, j : j + 1], (SUB, TILE)) for j in range(SUB)] for t in tiles
    ]
    left = []
    for t in tiles:
        a1, a2, a3 = pieces(panels[t], 3)
        left.append(jnp.concatenate([a1, a1, a2, a1, a2, a3], axis=0).astype(jnp.bfloat16))
    columns = swept(columns, subs)
    rows = []
    for t in tiles:
        source = jnp.where(inside, unit, -panels[t])
        terms = [columns[t][j] * jnp.broadcast_to(source[j : j + 1, :], (SUB, TILE)) for j in range(SUB)]
        while len(terms) > 1:
            terms = [terms[i] + terms[i + 1] for i in range(0, len(terms), 2)]
        rows.append(terms[0])
    changes = []
    for t in tiles:
        b1, b2, b3 = pieces(rows[t], 3)
        right = jnp.concatenate([b1, b2, b1, b3, b2, b1], axis=0).astype(jnp.bfloat16)
        changes.append(
            lax.dot_general(left[t], right, (((0,), (0,)), ((), ())), preferred_element_type=jnp.float32)
        )
    for t in tiles:
        ref[base + t] = jnp.where(outside, ref[base + t], 0.0) - changes[t]
        ref[base + t, pl.ds(first, SUB), :] = rows[t]


def split(x):
    high = x.astype(jnp.bfloat16)
    return high, (x - high.astype(jnp.float32)).astype(jnp.bfloat16)


def product(a, b):
    return jnp.dot(a, b, preferred_element_type=jnp.float32)


def dot(a, b):
    (ah, al), (bh, bl) = split(a), split(b)
    return product(ah, bh) + (product(ah, bl) + product(al, bh))


def body(
    slabs,
    reduce_here,
    pattern_ref,
    diagonal_hbm,
    lower_hbm,
    upper_hbm,
    ids_hbm,
    values_hbm,
    warm_hbm,
    boundary_hbm,
    modes_hbm,
    reduced_hbm,
    lower_ref,
    upper_ref,
    ids_ref,
    values_ref,
    warm_ref,
    boundary_ref,
    modes_ref,
    reduced_ref,
    local,
    lu,
    inv,
    halo,
    mid,
    parts,
    near_in,
    far_out,
    far_in,
    pair_send,
    pair_recv,
    halo_send,
    halo_recv,
    near_send,
    near_recv,
    far_send,
    far_recv,
):
    slab, col = lax.axis_index("slab"), lax.axis_index("col")
    here = lower_ref.shape[0]
    blocks = 2 * here
    width = warm_ref.shape[1]
    other = (slab, 1 - col)
    far = slabs // NEAR
    owned = IFACE // slabs
    hi, lo = slab // NEAR, lax.rem(slab, NEAR)
    near_ids = [(hi * NEAR + lax.rem(lo + k, NEAR), col) for k in range(1, NEAR)]
    far_ids = [(lax.rem(hi + k, far) * NEAR + lo, col) for k in range(1, far)]
    is_first, is_last = slab == 0, slab == slabs - 1

    barrier = pltpu.get_barrier_semaphore()
    steps = range(1, slabs) if reduce_here else (1, slabs - 1)
    partners = [other] + [(lax.rem(slab + k, slabs), col) for k in steps]
    for partner in partners:
        pl.semaphore_signal(barrier, inc=1, device_id=partner, device_id_type=MESH)

    mine = pl.ds(col * here, here)
    sources = [diagonal_hbm, lower_hbm, upper_hbm, warm_hbm, ids_hbm, values_hbm, boundary_hbm]
    places = [inv.at[mine], lower_ref, upper_ref, warm_ref, ids_ref, values_ref, boundary_ref]
    loads = [
        pltpu.make_async_copy(source, place, local.at[i])
        for i, (source, place) in enumerate(zip(sources, places))
    ]
    for load in loads:
        load.start()
    loads[1].wait()
    loads[2].wait()
    for b in range(here):
        at = col * here + b
        lu[at, :, :TILE] = lower_ref[b] * pattern_ref[b, 0].astype(jnp.float32)
        lu[at, :, TILE:] = upper_ref[b] * pattern_ref[b, 1].astype(jnp.float32)

    def halos(step, first_block, last_block):
        down = pltpu.make_async_remote_copy(
            src_ref=first_block,
            dst_ref=halo.at[2 * step + 1],
            send_sem=halo_send.at[2 * step],
            recv_sem=halo_recv.at[2 * step + 1],
            device_id=(slab - 1, col),
            device_id_type=MESH,
        )
        up = pltpu.make_async_remote_copy(
            src_ref=last_block,
            dst_ref=halo.at[2 * step],
            send_sem=halo_send.at[2 * step + 1],
            recv_sem=halo_recv.at[2 * step],
            device_id=(slab + 1, col),
            device_id_type=MESH,
        )
        return down, up

    def start_halos(copies):
        down, up = copies

        @pl.when(jnp.logical_not(is_first))
        def _():
            down.start()

        @pl.when(jnp.logical_not(is_last))
        def _():
            up.start()

    def wait_halos(step, copies):
        down, up = copies

        @pl.when(jnp.logical_not(is_first))
        def _():
            down.wait_send()
            up.wait_recv()

        @pl.when(is_first)
        def _():
            halo[2 * step] = jnp.zeros((TILE, width), jnp.float32)

        @pl.when(jnp.logical_not(is_last))
        def _():
            up.wait_send()
            down.wait_recv()

        @pl.when(is_last)
        def _():
            halo[2 * step + 1] = jnp.zeros((TILE, width), jnp.float32)

    def pair(ref, which):
        part = ref.at[mine]
        return pltpu.make_async_remote_copy(
            src_ref=part,
            dst_ref=part,
            send_sem=pair_send.at[which],
            recv_sem=pair_recv.at[which],
            device_id=other,
            device_id_type=MESH,
        )

    warm_halos = halos(0, warm_hbm.at[pl.ds(0, TILE)], warm_hbm.at[pl.ds((blocks - 1) * TILE, TILE)])
    tiles = pair(lu, 0)
    rows = blocks * TILE
    loads[0].wait()

    def invert(k, carry):
        sweep_rows(inv, col * here, here, k)
        return carry

    early = TILE // SUB // 4
    lax.fori_loop(0, early, invert, 0)
    pl.semaphore_wait(barrier, len(partners))
    start_halos(warm_halos)
    tiles.start()
    lax.fori_loop(early, TILE // SUB, invert, 0)
    inverses = pair(inv, 1)
    inverses.start()

    for load in loads[3:]:
        load.wait()
    ids_row = jnp.minimum(ids_ref[...], IFACE).astype(jnp.float32)
    ids_col = jnp.broadcast_to(ids_row, (8, rows)).T[:, :1].astype(jnp.int32)
    values_col = jnp.broadcast_to(values_ref[...], (8, rows)).T[:, :1]
    columns = lax.broadcasted_iota(jnp.int32, (TILE, width), 1) + col * width

    def right_side(b):
        part = slice(b * TILE, (b + 1) * TILE)
        return jnp.where(ids_col[part] == columns, -values_col[part], 0.0)

    def residual(b, below, above):
        both = jnp.concatenate([below, above], axis=0)
        return dot(lu[b], both) - right_side(b)

    def old(ref, step, b):
        if b < 0:
            return halo[2 * step]
        if b >= blocks:
            return halo[2 * step + 1]
        return ref[b * TILE : (b + 1) * TILE, :]

    tiles.wait()
    wait_halos(0, warm_halos)
    mid_halos = halos(1, mid.at[pl.ds(0, TILE)], mid.at[pl.ds((blocks - 1) * TILE, TILE)])
    order = [0, blocks - 1] + list(range(1, blocks - 1))
    held = [residual(b, old(warm_ref, 0, b - 1), old(warm_ref, 0, b + 1)) for b in order]
    inverses.wait()
    for n, b in enumerate(order):
        mid[b * TILE : (b + 1) * TILE, :] = dot(inv[b], held[n])
        if n == 1:
            start_halos(mid_halos)
    stores = []
    for n, b in enumerate(order[2:] + order[:2]):
        if n == blocks - 2:
            wait_halos(1, mid_halos)
        part = pl.ds(b * TILE, TILE)
        modes_ref[part, :] = dot(inv[b], residual(b, old(mid, 1, b - 1), old(mid, 1, b + 1)))
        store = pltpu.make_async_copy(modes_ref.at[part], modes_hbm.at[part], local.at[len(loads) + n])
        store.start()
        stores.append(store)

    ids_now = ids_row.astype(jnp.int32)
    weighted_high, weighted_low = split(values_col * modes_ref[...])
    group = IFACE // NEAR
    index = lax.broadcasted_iota(jnp.int32, (group, rows), 0)

    def pick(target):
        return jnp.where(index_target(target) == ids_now, 1.0, 0.0).astype(jnp.bfloat16)

    def share(chosen, part=slice(None)):
        return product(chosen, weighted_high[:, part]) + product(chosen, weighted_low[:, part])

    def index_target(target):
        if not reduce_here:
            return index + target * group
        return (index // owned) * (NEAR * owned) + target * owned + lax.rem(index, owned)

    def finish():
        last = pltpu.make_async_copy(reduced_ref, reduced_hbm, local.at[len(loads) + blocks])
        last.start()
        for store in stores + [last]:
            store.wait()

    if not reduce_here:
        for k in range(NEAR):
            reduced_ref[k * group : (k + 1) * group, :] = share(pick(k))
        finish()
        return

    half = width // 2
    halves = [slice(0, half), slice(half, width)]
    chosen = [pick(lax.rem(lo + k, NEAR)) for k in range(NEAR)]
    near_sent = []
    for h, part in enumerate(halves):
        for k in range(1, NEAR):
            parts[h, k - 1] = share(chosen[k], part)
            copy = pltpu.make_async_remote_copy(
                src_ref=parts.at[h, k - 1],
                dst_ref=near_in.at[h, k - 1],
                send_sem=near_send.at[h, k - 1],
                recv_sem=near_recv.at[h, k - 1],
                device_id=near_ids[k - 1],
                device_id_type=MESH,
            )
            copy.start()
            near_sent.append(copy)
    totals = [share(chosen[0], part) for part in halves]
    far_sent = []
    for h in range(2):
        total = totals[h]
        for k in range(NEAR - 1):
            near_sent[h * (NEAR - 1) + k].wait()
            total = total + near_in[h, k]
        far_out[h] = total.reshape(far, owned, half)
        for k in range(1, far):
            copy = pltpu.make_async_remote_copy(
                src_ref=far_out.at[h, lax.rem(hi + k, far)],
                dst_ref=far_in.at[h, k - 1],
                send_sem=far_send.at[h, k - 1],
                recv_sem=far_recv.at[h, k - 1],
                device_id=far_ids[k - 1],
                device_id_type=MESH,
            )
            copy.start()
            far_sent.append(copy)
    for h, part in enumerate(halves):
        result = boundary_ref[:, part] + far_out[h, hi]
        for k in range(far - 1):
            far_sent[h * (far - 1) + k].wait()
            result = result + far_in[h, k]
        reduced_ref[:, part] = result
    finish()


def on_device(
    diagonal_tiles,
    lower_tiles,
    upper_tiles,
    tile_pattern,
    interface_ids,
    coupling_values,
    warm_start,
    boundary_stiffness,
):
    slabs = lax.axis_size("slab")
    here = diagonal_tiles.shape[0]
    rows, width = warm_start.shape
    owned = boundary_stiffness.shape[0]
    reduce_here = slabs % NEAR == 0 and slabs > NEAR and owned % 8 == 0
    far = slabs // NEAR if reduce_here else 2
    hbm = pl.BlockSpec(memory_space=pltpu.HBM)
    f32 = jnp.float32
    sem = pltpu.SemaphoreType.DMA
    modes, reduced = pl.pallas_call(
        functools.partial(body, slabs, reduce_here),
        out_shape=(
            jax.ShapeDtypeStruct((rows, width), f32),
            jax.ShapeDtypeStruct((owned if reduce_here else IFACE, width), f32),
        ),
        in_specs=[pl.BlockSpec(memory_space=pltpu.SMEM)] + [hbm] * 7,
        out_specs=(hbm, hbm),
        scratch_shapes=[
            pltpu.VMEM((here, TILE, TILE), f32),
            pltpu.VMEM((here, TILE, TILE), f32),
            pltpu.VMEM((1, rows), jnp.int32),
            pltpu.VMEM((1, rows), f32),
            pltpu.VMEM((rows, width), f32),
            pltpu.VMEM((owned, width), f32),
            pltpu.VMEM((rows, width), f32),
            pltpu.VMEM((owned if reduce_here else IFACE, width), f32),
            sem((8 + 2 * here,)),
            pltpu.VMEM((2 * here, TILE, 2 * TILE), f32),
            pltpu.VMEM((2 * here, TILE, TILE), f32),
            pltpu.VMEM((2 * SWEEPS, TILE, width), f32),
            pltpu.VMEM((rows, width), f32),
            pltpu.VMEM((2, NEAR - 1, IFACE // NEAR, width // 2), f32),
            pltpu.VMEM((2, NEAR - 1, IFACE // NEAR, width // 2), f32),
            pltpu.VMEM((2, far, owned, width // 2), f32),
            pltpu.VMEM((2, far - 1, owned, width // 2), f32),
            sem((2,)),
            sem((2,)),
            sem((2 * SWEEPS,)),
            sem((2 * SWEEPS,)),
            sem((2, NEAR - 1)),
            sem((2, NEAR - 1)),
            sem((2, far - 1)),
            sem((2, far - 1)),
        ],
        compiler_params=pltpu.CompilerParams(
            collective_id=0, has_side_effects=True, vmem_limit_bytes=40 * 1024 * 1024
        ),
    )(
        tile_pattern,
        diagonal_tiles,
        lower_tiles,
        upper_tiles,
        interface_ids.reshape(1, rows),
        coupling_values.reshape(1, rows),
        warm_start,
        boundary_stiffness,
    )
    if not reduce_here:
        total = lax.psum(reduced, "slab")
        share = lax.dynamic_slice_in_dim(total, lax.axis_index("slab") * owned, owned)
        reduced = boundary_stiffness + share
    return (modes, reduced)


def solution(mesh):
    placed = (
        P(("slab", "col"), None, None),
        P(("slab", "col"), None, None),
        P(("slab", "col"), None, None),
        P(("slab", "col"), None),
        P("slab"),
        P("slab"),
        P("slab", "col"),
        P("slab", "col"),
    )
    return jax.shard_map(
        on_device,
        mesh=mesh,
        in_specs=placed,
        out_specs=(P("slab", "col"), P("slab", "col")),
        check_vma=False,
    )
```

```python
import functools

import jax
import jax.numpy as jnp
from jax import lax
from jax.experimental import pallas as pl
from jax.experimental.pallas import tpu as pltpu
from jax.sharding import PartitionSpec as P

IFACE = 512
TILE = 128
SWEEPS = 2
NEAR = 4
SUB = 8
MESH = pl.DeviceIdType.MESH


def pieces(x, count):
    out = []
    for _ in range(count):
        piece = x.astype(jnp.bfloat16).astype(jnp.float32)
        out.append(piece)
        x = x - piece
    return out


def swept(columns, subs):
    tiles = range(len(columns))
    for k in range(SUB):
        pivots = [[jnp.broadcast_to(columns[t][k][j : j + 1, :], (SUB, TILE)) for j in range(SUB)] for t in tiles]
        inverted = [1.0 / pivots[t][k] for t in tiles]
        scaled = [columns[t][k] * inverted[t] for t in tiles]
        here = subs == k
        new = []
        for t in tiles:
            new.append(
                [
                    jnp.where(here, -inverted[t], scaled[t])
                    if j == k
                    else jnp.where(here, pivots[t][j] * inverted[t], columns[t][j] - scaled[t] * pivots[t][j])
                    for j in range(SUB)
                ]
            )
        columns = new
    return columns


def sweep_rows(ref, base, count, k):
    first = pl.multiple_of(k * SUB, SUB)
    tiles = range(count)
    lanes = lax.broadcasted_iota(jnp.int32, (SUB, TILE), 1) - k * SUB
    subs = lax.broadcasted_iota(jnp.int32, (SUB, TILE), 0)
    inside = (lanes >= 0) & (lanes < SUB)
    unit = jnp.where(lanes == subs, 1.0, 0.0)
    full = lax.broadcasted_iota(jnp.int32, (TILE, TILE), 1) - k * SUB
    outside = (full < 0) | (full >= SUB)
    panels = [ref[base + t, pl.ds(first, SUB), :] for t in tiles]
    shift = lax.rem(TILE - k * SUB, TILE)
    corners = [pltpu.roll(panels[t], shift, 1) for t in tiles]
    columns = [
        [jnp.broadcast_to(corners[t][:, j : j + 1], (SUB, TILE)) for j in range(SUB)] for t in tiles
    ]
    left = []
    for t in tiles:
        a1, a2, a3 = pieces(panels[t], 3)
        left.append(jnp.concatenate([a1, a1, a2, a1, a2, a3], axis=0).astype(jnp.bfloat16))
    columns = swept(columns, subs)
    rows = []
    for t in tiles:
        source = jnp.where(inside, unit, -panels[t])
        terms = [columns[t][j] * jnp.broadcast_to(source[j : j + 1, :], (SUB, TILE)) for j in range(SUB)]
        while len(terms) > 1:
            terms = [terms[i] + terms[i + 1] for i in range(0, len(terms), 2)]
        rows.append(terms[0])
    changes = []
    for t in tiles:
        b1, b2, b3 = pieces(rows[t], 3)
        right = jnp.concatenate([b1, b2, b1, b3, b2, b1], axis=0).astype(jnp.bfloat16)
        changes.append(
            lax.dot_general(left[t], right, (((0,), (0,)), ((), ())), preferred_element_type=jnp.float32)
        )
    for t in tiles:
        ref[base + t] = jnp.where(outside, ref[base + t], 0.0) - changes[t]
        ref[base + t, pl.ds(first, SUB), :] = rows[t]


def split(x):
    high = x.astype(jnp.bfloat16)
    return high, (x - high.astype(jnp.float32)).astype(jnp.bfloat16)


def product(a, b):
    return jnp.dot(a, b, preferred_element_type=jnp.float32)


def dot(a, b):
    (ah, al), (bh, bl) = split(a), split(b)
    return product(ah, bh) + (product(ah, bl) + product(al, bh))


def body(
    slabs,
    reduce_here,
    pattern_ref,
    diagonal_hbm,
    lower_hbm,
    upper_hbm,
    ids_hbm,
    values_hbm,
    warm_hbm,
    boundary_hbm,
    modes_ref,
    reduced_ref,
    lower_ref,
    upper_ref,
    ids_ref,
    values_ref,
    warm_ref,
    boundary_ref,
    local,
    lu,
    inv,
    halo,
    mid,
    parts,
    near_in,
    far_out,
    far_in,
    pair_send,
    pair_recv,
    halo_send,
    halo_recv,
    near_send,
    near_recv,
    far_send,
    far_recv,
):
    slab, col = lax.axis_index("slab"), lax.axis_index("col")
    here = lower_ref.shape[0]
    blocks = 2 * here
    width = warm_ref.shape[1]
    other = (slab, 1 - col)
    far = slabs // NEAR
    owned = IFACE // slabs
    hi, lo = slab // NEAR, lax.rem(slab, NEAR)
    near_ids = [(hi * NEAR + lax.rem(lo + k, NEAR), col) for k in range(1, NEAR)]
    far_ids = [(lax.rem(hi + k, far) * NEAR + lo, col) for k in range(1, far)]
    is_first, is_last = slab == 0, slab == slabs - 1

    barrier = pltpu.get_barrier_semaphore()
    steps = range(1, slabs) if reduce_here else (1, slabs - 1)
    partners = [other] + [(lax.rem(slab + k, slabs), col) for k in steps]
    for partner in partners:
        pl.semaphore_signal(barrier, inc=1, device_id=partner, device_id_type=MESH)

    mine = pl.ds(col * here, here)
    sources = [diagonal_hbm, lower_hbm, upper_hbm, warm_hbm, ids_hbm, values_hbm, boundary_hbm]
    places = [inv.at[mine], lower_ref, upper_ref, warm_ref, ids_ref, values_ref, boundary_ref]
    loads = [
        pltpu.make_async_copy(source, place, local.at[i])
        for i, (source, place) in enumerate(zip(sources, places))
    ]
    for load in loads:
        load.start()
    loads[1].wait()
    loads[2].wait()
    for b in range(here):
        at = col * here + b
        lu[at, :, :TILE] = lower_ref[b] * pattern_ref[b, 0].astype(jnp.float32)
        lu[at, :, TILE:] = upper_ref[b] * pattern_ref[b, 1].astype(jnp.float32)

    def halos(step, first_block, last_block):
        down = pltpu.make_async_remote_copy(
            src_ref=first_block,
            dst_ref=halo.at[2 * step + 1],
            send_sem=halo_send.at[2 * step],
            recv_sem=halo_recv.at[2 * step + 1],
            device_id=(slab - 1, col),
            device_id_type=MESH,
        )
        up = pltpu.make_async_remote_copy(
            src_ref=last_block,
            dst_ref=halo.at[2 * step],
            send_sem=halo_send.at[2 * step + 1],
            recv_sem=halo_recv.at[2 * step],
            device_id=(slab + 1, col),
            device_id_type=MESH,
        )
        return down, up

    def start_halos(copies):
        down, up = copies

        @pl.when(jnp.logical_not(is_first))
        def _():
            down.start()

        @pl.when(jnp.logical_not(is_last))
        def _():
            up.start()

    def wait_halos(step, copies):
        down, up = copies

        @pl.when(jnp.logical_not(is_first))
        def _():
            down.wait_send()
            up.wait_recv()

        @pl.when(is_first)
        def _():
            halo[2 * step] = jnp.zeros((TILE, width), jnp.float32)

        @pl.when(jnp.logical_not(is_last))
        def _():
            up.wait_send()
            down.wait_recv()

        @pl.when(is_last)
        def _():
            halo[2 * step + 1] = jnp.zeros((TILE, width), jnp.float32)

    def pair(ref, which):
        part = ref.at[mine]
        return pltpu.make_async_remote_copy(
            src_ref=part,
            dst_ref=part,
            send_sem=pair_send.at[which],
            recv_sem=pair_recv.at[which],
            device_id=other,
            device_id_type=MESH,
        )

    warm_halos = halos(0, warm_hbm.at[pl.ds(0, TILE)], warm_hbm.at[pl.ds((blocks - 1) * TILE, TILE)])
    tiles = pair(lu, 0)
    rows = blocks * TILE
    loads[0].wait()

    def invert(k, carry):
        sweep_rows(inv, col * here, here, k)
        return carry

    early = TILE // SUB // 4
    lax.fori_loop(0, early, invert, 0)
    pl.semaphore_wait(barrier, len(partners))
    start_halos(warm_halos)
    tiles.start()
    lax.fori_loop(early, TILE // SUB, invert, 0)
    inverses = pair(inv, 1)
    inverses.start()

    for load in loads[3:]:
        load.wait()
    ids_row = jnp.minimum(ids_ref[...], IFACE).astype(jnp.float32)
    ids_col = jnp.broadcast_to(ids_row, (8, rows)).T[:, :1].astype(jnp.int32)
    values_col = jnp.broadcast_to(values_ref[...], (8, rows)).T[:, :1]
    columns = lax.broadcasted_iota(jnp.int32, (TILE, width), 1) + col * width

    def right_side(b):
        part = slice(b * TILE, (b + 1) * TILE)
        return jnp.where(ids_col[part] == columns, -values_col[part], 0.0)

    def residual(b, below, above):
        both = jnp.concatenate([below, above], axis=0)
        return dot(lu[b], both) - right_side(b)

    def old(ref, step, b):
        if b < 0:
            return halo[2 * step]
        if b >= blocks:
            return halo[2 * step + 1]
        return ref[b * TILE : (b + 1) * TILE, :]

    tiles.wait()
    wait_halos(0, warm_halos)
    mid_halos = halos(1, mid.at[pl.ds(0, TILE)], mid.at[pl.ds((blocks - 1) * TILE, TILE)])
    order = [0, blocks - 1] + list(range(1, blocks - 1))
    held = [residual(b, old(warm_ref, 0, b - 1), old(warm_ref, 0, b + 1)) for b in order]
    inverses.wait()
    for n, b in enumerate(order):
        mid[b * TILE : (b + 1) * TILE, :] = dot(inv[b], held[n])
        if n == 1:
            start_halos(mid_halos)
    for n, b in enumerate(order[2:] + order[:2]):
        if n == blocks - 2:
            wait_halos(1, mid_halos)
        part = pl.ds(b * TILE, TILE)
        modes_ref[part, :] = dot(inv[b], residual(b, old(mid, 1, b - 1), old(mid, 1, b + 1)))

    ids_now = ids_row.astype(jnp.int32)
    weighted_high, weighted_low = split(values_col * modes_ref[...])
    group = IFACE // NEAR
    index = lax.broadcasted_iota(jnp.int32, (group, rows), 0)

    def pick(target):
        return jnp.where(index_target(target) == ids_now, 1.0, 0.0).astype(jnp.bfloat16)

    def share(chosen, part=slice(None)):
        return product(chosen, weighted_high[:, part]) + product(chosen, weighted_low[:, part])

    def index_target(target):
        if not reduce_here:
            return index + target * group
        return (index // owned) * (NEAR * owned) + target * owned + lax.rem(index, owned)

    if not reduce_here:
        for k in range(NEAR):
            reduced_ref[k * group : (k + 1) * group, :] = share(pick(k))
        return

    half = width // 2
    halves = [slice(0, half), slice(half, width)]
    chosen = [pick(lax.rem(lo + k, NEAR)) for k in range(NEAR)]
    near_sent = []
    for h, part in enumerate(halves):
        for k in range(1, NEAR):
            parts[h, k - 1] = share(chosen[k], part)
            copy = pltpu.make_async_remote_copy(
                src_ref=parts.at[h, k - 1],
                dst_ref=near_in.at[h, k - 1],
                send_sem=near_send.at[h, k - 1],
                recv_sem=near_recv.at[h, k - 1],
                device_id=near_ids[k - 1],
                device_id_type=MESH,
            )
            copy.start()
            near_sent.append(copy)
    totals = [share(chosen[0], part) for part in halves]
    far_sent = []
    for h in range(2):
        total = totals[h]
        for k in range(NEAR - 1):
            near_sent[h * (NEAR - 1) + k].wait()
            total = total + near_in[h, k]
        far_out[h] = total.reshape(far, owned, half)
        for k in range(1, far):
            copy = pltpu.make_async_remote_copy(
                src_ref=far_out.at[h, lax.rem(hi + k, far)],
                dst_ref=far_in.at[h, k - 1],
                send_sem=far_send.at[h, k - 1],
                recv_sem=far_recv.at[h, k - 1],
                device_id=far_ids[k - 1],
                device_id_type=MESH,
            )
            copy.start()
            far_sent.append(copy)
    for h, part in enumerate(halves):
        result = boundary_ref[:, part] + far_out[h, hi]
        for k in range(far - 1):
            far_sent[h * (far - 1) + k].wait()
            result = result + far_in[h, k]
        reduced_ref[:, part] = result


def on_device(
    diagonal_tiles,
    lower_tiles,
    upper_tiles,
    tile_pattern,
    interface_ids,
    coupling_values,
    warm_start,
    boundary_stiffness,
):
    slabs = lax.axis_size("slab")
    here = diagonal_tiles.shape[0]
    rows, width = warm_start.shape
    owned = boundary_stiffness.shape[0]
    reduce_here = slabs % NEAR == 0 and slabs > NEAR and owned % 8 == 0
    far = slabs // NEAR if reduce_here else 2
    hbm = pl.BlockSpec(memory_space=pltpu.HBM)
    f32 = jnp.float32
    sem = pltpu.SemaphoreType.DMA
    modes, reduced = pl.pallas_call(
        functools.partial(body, slabs, reduce_here),
        out_shape=(
            jax.ShapeDtypeStruct((rows, width), f32),
            jax.ShapeDtypeStruct((owned if reduce_here else IFACE, width), f32),
        ),
        in_specs=[pl.BlockSpec(memory_space=pltpu.SMEM)] + [hbm] * 7,
        out_specs=(pl.BlockSpec(memory_space=pltpu.VMEM),) * 2,
        scratch_shapes=[
            pltpu.VMEM((here, TILE, TILE), f32),
            pltpu.VMEM((here, TILE, TILE), f32),
            pltpu.VMEM((1, rows), jnp.int32),
            pltpu.VMEM((1, rows), f32),
            pltpu.VMEM((rows, width), f32),
            pltpu.VMEM((owned, width), f32),
            sem((7,)),
            pltpu.VMEM((2 * here, TILE, 2 * TILE), f32),
            pltpu.VMEM((2 * here, TILE, TILE), f32),
            pltpu.VMEM((2 * SWEEPS, TILE, width), f32),
            pltpu.VMEM((rows, width), f32),
            pltpu.VMEM((2, NEAR - 1, IFACE // NEAR, width // 2), f32),
            pltpu.VMEM((2, NEAR - 1, IFACE // NEAR, width // 2), f32),
            pltpu.VMEM((2, far, owned, width // 2), f32),
            pltpu.VMEM((2, far - 1, owned, width // 2), f32),
            sem((2,)),
            sem((2,)),
            sem((2 * SWEEPS,)),
            sem((2 * SWEEPS,)),
            sem((2, NEAR - 1)),
            sem((2, NEAR - 1)),
            sem((2, far - 1)),
            sem((2, far - 1)),
        ],
        compiler_params=pltpu.CompilerParams(
            collective_id=0, has_side_effects=True, vmem_limit_bytes=40 * 1024 * 1024
        ),
    )(
        *(
            pltpu.with_memory_space_constraint(x, pltpu.HBM)
            for x in (
                tile_pattern,
                diagonal_tiles,
                lower_tiles,
                upper_tiles,
                interface_ids.reshape(1, rows),
                coupling_values.reshape(1, rows),
                warm_start,
                boundary_stiffness,
            )
        ),
    )
    if not reduce_here:
        total = lax.psum(reduced, "slab")
        share = lax.dynamic_slice_in_dim(total, lax.axis_index("slab") * owned, owned)
        reduced = boundary_stiffness + share
    return (modes, reduced)


def solution(mesh):
    placed = (
        P(("slab", "col"), None, None),
        P(("slab", "col"), None, None),
        P(("slab", "col"), None, None),
        P(("slab", "col"), None),
        P("slab"),
        P("slab"),
        P("slab", "col"),
        P("slab", "col"),
    )
    return jax.shard_map(
        on_device,
        mesh=mesh,
        in_specs=placed,
        out_specs=(P("slab", "col"), P("slab", "col")),
        check_vma=False,
    )
```

```python
import functools

import jax
import jax.numpy as jnp
from jax import lax
from jax.experimental import pallas as pl
from jax.experimental.pallas import tpu as pltpu
from jax.sharding import PartitionSpec as P

IFACE = 512
TILE = 128
SWEEPS = 2
NEAR = 4
SUB = 8
MESH = pl.DeviceIdType.MESH


def pieces(x, count):
    out = []
    for _ in range(count):
        piece = x.astype(jnp.bfloat16).astype(jnp.float32)
        out.append(piece)
        x = x - piece
    return out


def swept(columns, subs):
    tiles = range(len(columns))
    for k in range(SUB):
        pivots = [[jnp.broadcast_to(columns[t][k][j : j + 1, :], (SUB, TILE)) for j in range(SUB)] for t in tiles]
        inverted = [1.0 / pivots[t][k] for t in tiles]
        scaled = [columns[t][k] * inverted[t] for t in tiles]
        here = subs == k
        new = []
        for t in tiles:
            new.append(
                [
                    jnp.where(here, -inverted[t], scaled[t])
                    if j == k
                    else jnp.where(here, pivots[t][j] * inverted[t], columns[t][j] - scaled[t] * pivots[t][j])
                    for j in range(SUB)
                ]
            )
        columns = new
    return columns


def sweep_rows(ref, base, count, k):
    first = pl.multiple_of(k * SUB, SUB)
    tiles = range(count)
    lanes = lax.broadcasted_iota(jnp.int32, (SUB, TILE), 1) - k * SUB
    subs = lax.broadcasted_iota(jnp.int32, (SUB, TILE), 0)
    inside = (lanes >= 0) & (lanes < SUB)
    unit = jnp.where(lanes == subs, 1.0, 0.0)
    full = lax.broadcasted_iota(jnp.int32, (TILE, TILE), 1) - k * SUB
    outside = (full < 0) | (full >= SUB)
    panels = [ref[base + t, pl.ds(first, SUB), :] for t in tiles]
    shift = lax.rem(TILE - k * SUB, TILE)
    corners = [pltpu.roll(panels[t], shift, 1) for t in tiles]
    columns = [
        [jnp.broadcast_to(corners[t][:, j : j + 1], (SUB, TILE)) for j in range(SUB)] for t in tiles
    ]
    left = []
    for t in tiles:
        a1, a2, a3 = pieces(panels[t], 3)
        left.append(jnp.concatenate([a1, a1, a2, a1, a2, a3], axis=0).astype(jnp.bfloat16))
    columns = swept(columns, subs)
    rows = []
    for t in tiles:
        source = jnp.where(inside, unit, -panels[t])
        terms = [columns[t][j] * jnp.broadcast_to(source[j : j + 1, :], (SUB, TILE)) for j in range(SUB)]
        while len(terms) > 1:
            terms = [terms[i] + terms[i + 1] for i in range(0, len(terms), 2)]
        rows.append(terms[0])
    changes = []
    for t in tiles:
        b1, b2, b3 = pieces(rows[t], 3)
        right = jnp.concatenate([b1, b2, b1, b3, b2, b1], axis=0).astype(jnp.bfloat16)
        changes.append(
            lax.dot_general(left[t], right, (((0,), (0,)), ((), ())), preferred_element_type=jnp.float32)
        )
    for t in tiles:
        ref[base + t] = jnp.where(outside, ref[base + t], 0.0) - changes[t]
        ref[base + t, pl.ds(first, SUB), :] = rows[t]


def split(x):
    high = x.astype(jnp.bfloat16)
    return high, (x - high.astype(jnp.float32)).astype(jnp.bfloat16)


def product(a, b):
    return jnp.dot(a, b, preferred_element_type=jnp.float32)


def dot(a, b):
    (ah, al), (bh, bl) = split(a), split(b)
    return product(ah, bh) + (product(ah, bl) + product(al, bh))


def body(
    slabs,
    reduce_here,
    pattern_ref,
    diagonal_hbm,
    lower_hbm,
    upper_hbm,
    ids_hbm,
    values_hbm,
    warm_hbm,
    boundary_hbm,
    modes_ref,
    reduced_ref,
    lower_ref,
    upper_ref,
    ids_ref,
    values_ref,
    warm_ref,
    boundary_ref,
    local,
    lu,
    inv,
    halo,
    mid,
    parts,
    near_in,
    far_out,
    far_in,
    pair_send,
    pair_recv,
    halo_send,
    halo_recv,
    near_send,
    near_recv,
    far_send,
    far_recv,
):
    slab, col = lax.axis_index("slab"), lax.axis_index("col")
    here = lower_ref.shape[0]
    blocks = 2 * here
    width = warm_ref.shape[1]
    other = (slab, 1 - col)
    far = slabs // NEAR
    owned = IFACE // slabs
    hi, lo = slab // NEAR, lax.rem(slab, NEAR)
    near_ids = [(hi * NEAR + lax.rem(lo + k, NEAR), col) for k in range(1, NEAR)]
    far_ids = [(lax.rem(hi + k, far) * NEAR + lo, col) for k in range(1, far)]
    is_first, is_last = slab == 0, slab == slabs - 1

    barrier = pltpu.get_barrier_semaphore()
    steps = range(1, slabs) if reduce_here else (1, slabs - 1)
    partners = [other] + [(lax.rem(slab + k, slabs), col) for k in steps]
    for partner in partners:
        pl.semaphore_signal(barrier, inc=1, device_id=partner, device_id_type=MESH)

    mine = pl.ds(col * here, here)
    sources = [diagonal_hbm, lower_hbm, upper_hbm, warm_hbm, ids_hbm, values_hbm, boundary_hbm]
    places = [inv.at[mine], lower_ref, upper_ref, warm_ref, ids_ref, values_ref, boundary_ref]
    loads = [
        pltpu.make_async_copy(source, place, local.at[i])
        for i, (source, place) in enumerate(zip(sources, places))
    ]
    for load in loads:
        load.start()
    def halos(step, first_block, last_block):
        down = pltpu.make_async_remote_copy(
            src_ref=first_block,
            dst_ref=halo.at[2 * step + 1],
            send_sem=halo_send.at[2 * step],
            recv_sem=halo_recv.at[2 * step + 1],
            device_id=(slab - 1, col),
            device_id_type=MESH,
        )
        up = pltpu.make_async_remote_copy(
            src_ref=last_block,
            dst_ref=halo.at[2 * step],
            send_sem=halo_send.at[2 * step + 1],
            recv_sem=halo_recv.at[2 * step],
            device_id=(slab + 1, col),
            device_id_type=MESH,
        )
        return down, up

    def start_halos(copies):
        down, up = copies

        @pl.when(jnp.logical_not(is_first))
        def _():
            down.start()

        @pl.when(jnp.logical_not(is_last))
        def _():
            up.start()

    def wait_halos(step, copies):
        down, up = copies

        @pl.when(jnp.logical_not(is_first))
        def _():
            down.wait_send()
            up.wait_recv()

        @pl.when(is_first)
        def _():
            halo[2 * step] = jnp.zeros((TILE, width), jnp.float32)

        @pl.when(jnp.logical_not(is_last))
        def _():
            up.wait_send()
            down.wait_recv()

        @pl.when(is_last)
        def _():
            halo[2 * step + 1] = jnp.zeros((TILE, width), jnp.float32)

    def pair(ref, which):
        part = ref.at[mine]
        return pltpu.make_async_remote_copy(
            src_ref=part,
            dst_ref=part,
            send_sem=pair_send.at[which],
            recv_sem=pair_recv.at[which],
            device_id=other,
            device_id_type=MESH,
        )

    warm_halos = halos(0, warm_hbm.at[pl.ds(0, TILE)], warm_hbm.at[pl.ds((blocks - 1) * TILE, TILE)])
    tiles = pair(lu, 0)
    rows = blocks * TILE
    loads[0].wait()

    def invert(k, carry):
        sweep_rows(inv, col * here, here, k)
        return carry

    early = TILE // SUB // 4
    lax.fori_loop(0, early, invert, 0)
    loads[1].wait()
    loads[2].wait()
    for b in range(here):
        at = col * here + b
        lu[at, :, :TILE] = lower_ref[b] * pattern_ref[b, 0].astype(jnp.float32)
        lu[at, :, TILE:] = upper_ref[b] * pattern_ref[b, 1].astype(jnp.float32)
    pl.semaphore_wait(barrier, len(partners))
    start_halos(warm_halos)
    tiles.start()
    lax.fori_loop(early, TILE // SUB, invert, 0)
    inverses = pair(inv, 1)
    inverses.start()

    for load in loads[3:]:
        load.wait()
    ids_row = jnp.minimum(ids_ref[...], IFACE).astype(jnp.float32)
    ids_col = jnp.broadcast_to(ids_row, (8, rows)).T[:, :1].astype(jnp.int32)
    values_col = jnp.broadcast_to(values_ref[...], (8, rows)).T[:, :1]
    columns = lax.broadcasted_iota(jnp.int32, (TILE, width), 1) + col * width

    def right_side(b):
        part = slice(b * TILE, (b + 1) * TILE)
        return jnp.where(ids_col[part] == columns, -values_col[part], 0.0)

    def residual(b, below, above):
        both = jnp.concatenate([below, above], axis=0)
        return dot(lu[b], both) - right_side(b)

    def old(ref, step, b):
        if b < 0:
            return halo[2 * step]
        if b >= blocks:
            return halo[2 * step + 1]
        return ref[b * TILE : (b + 1) * TILE, :]

    tiles.wait()
    wait_halos(0, warm_halos)
    mid_halos = halos(1, mid.at[pl.ds(0, TILE)], mid.at[pl.ds((blocks - 1) * TILE, TILE)])
    order = [0, blocks - 1] + list(range(1, blocks - 1))
    held = [residual(b, old(warm_ref, 0, b - 1), old(warm_ref, 0, b + 1)) for b in order]
    inverses.wait()
    for n, b in enumerate(order):
        mid[b * TILE : (b + 1) * TILE, :] = dot(inv[b], held[n])
        if n == 1:
            start_halos(mid_halos)
    ids_now = ids_row.astype(jnp.int32)
    group = IFACE // NEAR
    index = lax.broadcasted_iota(jnp.int32, (group, rows), 0)

    def index_target(target):
        if not reduce_here:
            return index + target * group
        return (index // owned) * (NEAR * owned) + target * owned + lax.rem(index, owned)

    def pick(target):
        return jnp.where(index_target(target) == ids_now, 1.0, 0.0).astype(jnp.bfloat16)

    chosen = [pick(lax.rem(lo + k, NEAR)) for k in range(NEAR)] if reduce_here else []
    for n, b in enumerate(order[2:] + order[:2]):
        if n == blocks - 2:
            wait_halos(1, mid_halos)
        part = pl.ds(b * TILE, TILE)
        modes_ref[part, :] = dot(inv[b], residual(b, old(mid, 1, b - 1), old(mid, 1, b + 1)))

    weighted_high, weighted_low = split(values_col * modes_ref[...])

    def share(chosen, part=slice(None)):
        return product(chosen, weighted_high[:, part]) + product(chosen, weighted_low[:, part])

    if not reduce_here:
        for k in range(NEAR):
            reduced_ref[k * group : (k + 1) * group, :] = share(pick(k))
        return

    half = width // 2
    halves = [slice(0, half), slice(half, width)]
    near_sent = []
    for h, part in enumerate(halves):
        for k in range(1, NEAR):
            parts[h, k - 1] = share(chosen[k], part)
            copy = pltpu.make_async_remote_copy(
                src_ref=parts.at[h, k - 1],
                dst_ref=near_in.at[h, k - 1],
                send_sem=near_send.at[h, k - 1],
                recv_sem=near_recv.at[h, k - 1],
                device_id=near_ids[k - 1],
                device_id_type=MESH,
            )
            copy.start()
            near_sent.append(copy)
    totals = [share(chosen[0], part) for part in halves]
    far_sent = []
    for h in range(2):
        total = totals[h]
        for k in range(NEAR - 1):
            near_sent[h * (NEAR - 1) + k].wait()
            total = total + near_in[h, k]
        far_out[h] = total.reshape(far, owned, half)
        for k in range(1, far):
            copy = pltpu.make_async_remote_copy(
                src_ref=far_out.at[h, lax.rem(hi + k, far)],
                dst_ref=far_in.at[h, k - 1],
                send_sem=far_send.at[h, k - 1],
                recv_sem=far_recv.at[h, k - 1],
                device_id=far_ids[k - 1],
                device_id_type=MESH,
            )
            copy.start()
            far_sent.append(copy)
    for h, part in enumerate(halves):
        result = boundary_ref[:, part] + far_out[h, hi]
        for k in range(far - 1):
            far_sent[h * (far - 1) + k].wait()
            result = result + far_in[h, k]
        reduced_ref[:, part] = result


def on_device(
    diagonal_tiles,
    lower_tiles,
    upper_tiles,
    tile_pattern,
    interface_ids,
    coupling_values,
    warm_start,
    boundary_stiffness,
):
    slabs = lax.axis_size("slab")
    here = diagonal_tiles.shape[0]
    rows, width = warm_start.shape
    owned = boundary_stiffness.shape[0]
    reduce_here = slabs % NEAR == 0 and slabs > NEAR and owned % 8 == 0
    far = slabs // NEAR if reduce_here else 2
    hbm = pl.BlockSpec(memory_space=pltpu.HBM)
    f32 = jnp.float32
    sem = pltpu.SemaphoreType.DMA
    modes, reduced = pl.pallas_call(
        functools.partial(body, slabs, reduce_here),
        out_shape=(
            jax.ShapeDtypeStruct((rows, width), f32),
            jax.ShapeDtypeStruct((owned if reduce_here else IFACE, width), f32),
        ),
        in_specs=[pl.BlockSpec(memory_space=pltpu.SMEM)] + [hbm] * 7,
        out_specs=(pl.BlockSpec(memory_space=pltpu.VMEM),) * 2,
        scratch_shapes=[
            pltpu.VMEM((here, TILE, TILE), f32),
            pltpu.VMEM((here, TILE, TILE), f32),
            pltpu.VMEM((1, rows), jnp.int32),
            pltpu.VMEM((1, rows), f32),
            pltpu.VMEM((rows, width), f32),
            pltpu.VMEM((owned, width), f32),
            sem((7,)),
            pltpu.VMEM((2 * here, TILE, 2 * TILE), f32),
            pltpu.VMEM((2 * here, TILE, TILE), f32),
            pltpu.VMEM((2 * SWEEPS, TILE, width), f32),
            pltpu.VMEM((rows, width), f32),
            pltpu.VMEM((2, NEAR - 1, IFACE // NEAR, width // 2), f32),
            pltpu.VMEM((2, NEAR - 1, IFACE // NEAR, width // 2), f32),
            pltpu.VMEM((2, far, owned, width // 2), f32),
            pltpu.VMEM((2, far - 1, owned, width // 2), f32),
            sem((2,)),
            sem((2,)),
            sem((2 * SWEEPS,)),
            sem((2 * SWEEPS,)),
            sem((2, NEAR - 1)),
            sem((2, NEAR - 1)),
            sem((2, far - 1)),
            sem((2, far - 1)),
        ],
        compiler_params=pltpu.CompilerParams(
            collective_id=0, has_side_effects=True, vmem_limit_bytes=40 * 1024 * 1024
        ),
    )(
        *(
            pltpu.with_memory_space_constraint(x, pltpu.HBM)
            for x in (
                tile_pattern,
                diagonal_tiles,
                lower_tiles,
                upper_tiles,
                interface_ids.reshape(1, rows),
                coupling_values.reshape(1, rows),
                warm_start,
                boundary_stiffness,
            )
        ),
    )
    if not reduce_here:
        total = lax.psum(reduced, "slab")
        share = lax.dynamic_slice_in_dim(total, lax.axis_index("slab") * owned, owned)
        reduced = boundary_stiffness + share
    return (modes, reduced)


def solution(mesh):
    placed = (
        P(("slab", "col"), None, None),
        P(("slab", "col"), None, None),
        P(("slab", "col"), None, None),
        P(("slab", "col"), None),
        P("slab"),
        P("slab"),
        P("slab", "col"),
        P("slab", "col"),
    )
    return jax.shard_map(
        on_device,
        mesh=mesh,
        in_specs=placed,
        out_specs=(P("slab", "col"), P("slab", "col")),
        check_vma=False,
    )
```
